256 devices in a mesh: row: 16 (over z, core), col: 16 (over x, y).
Axes of the slice: x: 4, y: 4, z: 8, core: 2. Of those that a mesh axis runs over, the one named last changes fastest.
Arguments:
- tokens: bfloat16 [2048, 6144], P('col', 'row'), may hold values from -6 to 6
- w_in: bfloat16 [6144, 24576], P('row', 'col'), may hold values from -0.078125 to 0.078125
- w_out: bfloat16 [24576, 6144], P('col', 'row'), may hold values from -0.0390625 to 0.0390625
- cotangent: bfloat16 [2048, 6144], P('col', 'row'), may hold values from -6 to 6
Outputs:
- mixed: bfloat16 [2048, 6144], P('col', 'row')
- grad_tokens: bfloat16 [2048, 6144], P('col', 'row')
- grad_w_in: float32 [6144, 24576], P('row', 'col')
- grad_w_out: float32 [24576, 6144], P('col', 'row')
The draws below stay inside these ranges and needn't reach their ends.
All inputs are finite; a program needn't handle non-finite values.
Results may differ from the reference program's by a relative error of at most 0.033.
Values may be sent and summed in bfloat16 or wider, within the bound.
No kernel may reach another device: no remote copies, remote signals or barrier semaphores. Data moves between devices by JAX's collectives and lax.ppermute only.
A program may use at most 128 MiB of HBM per device.

```python
import math
import jax
import jax.numpy as jnp
from jax import lax

D = 6144
FF = 24576
TOKENS = 2048
N_ROW = 16
N_COL = 16


def block_levels(key, shape, pieces, smallest, top_value):
    level = 1.0
    for axis_at, blocks in pieces:
        steps = jax.random.uniform(jax.random.fold_in(jax.random.fold_in(key, 6), axis_at), (blocks,), jnp.float32, smallest / len(pieces), top_value / len(pieces))
        level = level * jnp.repeat(jnp.exp(steps), shape[axis_at] // blocks).reshape((-1,) + (1,) * (len(shape) - 1 - axis_at))
    return level


def gaussian(stream_key, extent, scale, most, pieces=(), held_as=jnp.bfloat16):
    drawn = jax.random.normal(stream_key, extent, jnp.float32) * scale
    if len(pieces) > 0:
        drawn = block_levels(stream_key, extent, pieces, -0.22, 0.18) * drawn
    return jnp.clip(drawn, min=-most, max=most).astype(held_as)


def setup_inputs(seed: int = 0) -> dict:
    key_of = jax.random.split(jax.random.key(seed), 5)
    tokens = gaussian(key_of[0], (TOKENS, D), 1.0, 6.0, ((0, 16), (1, 16)))
    w_in = gaussian(key_of[1], (D, FF), D ** -0.5, 0.078125, ((0, 16), (1, 16)))
    w_out = gaussian(key_of[2], (FF, D), FF ** -0.5, 0.0390625, ((0, 16), (1, 16)))
    cotangent = gaussian(key_of[3], (TOKENS, D), 1.0, 6.0, ((0, 16), (1, 16)))
    return dict(tokens=tokens, w_in=w_in, w_out=w_out, cotangent=cotangent)


def gelu_value(v):
    return v * 0.5 * (1.0 + lax.erf(v / math.sqrt(2.0)))

def gelu_slope(v):
    return 0.5 * (1.0 + lax.erf(v / math.sqrt(2.0))) + v * jnp.exp(-0.5 * v * v) / math.sqrt(2.0 * math.pi)

def block_product(left, right, count):
    width = left.shape[1] // count

    def step(total, index):
        start = (index * width).astype(jnp.int32)
        piece_a = lax.dynamic_slice_in_dim(left, start, width, 1)
        piece_b = lax.dynamic_slice_in_dim(right, start, width, 0)
        partial_value = jnp.dot(piece_a, piece_b, preferred_element_type=jnp.float32).astype(jnp.bfloat16)
        partial_value = lax.optimization_barrier(partial_value)
        return (total + partial_value.astype(jnp.float32), None)
    empty = jnp.zeros((left.shape[0], right.shape[1]), jnp.float32)
    total, _ = lax.scan(step, empty, jnp.arange(count, dtype=jnp.int32))
    return total

def reference(tokens, w_in, w_out, cotangent):
    pre = block_product(tokens, w_in, N_ROW)
    hidden = gelu_value(pre).astype(jnp.bfloat16)
    mixed = block_product(hidden, w_out, N_COL).astype(jnp.bfloat16)
    grad_hidden = block_product(cotangent, w_out.T, N_ROW)
    grad_pre = (grad_hidden * gelu_slope(pre)).astype(jnp.bfloat16)
    grad_tokens = block_product(grad_pre, w_in.T, N_COL).astype(jnp.bfloat16)
    factor = 1.0 / math.sqrt(TOKENS)
    grad_w_in = jnp.dot(tokens.T, grad_pre, preferred_element_type=jnp.float32) * factor
    grad_w_out = jnp.dot(hidden.T, cotangent, preferred_element_type=jnp.float32) * factor
    return (mixed, grad_tokens, grad_w_in, grad_w_out)
```

```python
import math

import jax
import jax.numpy as jnp
from jax import lax
from jax.sharding import PartitionSpec as P

BF = jnp.bfloat16
F32 = jnp.float32
ROWS, COLS = 16, 16
SWAP = [(r, r ^ 1) for r in range(ROWS)]
SAME_CORE = [[2 * z + k for z in range(ROWS // 2)] for k in range(2)]
CONTRACT_ROWS = (((0,), (0,)), ((), ()))
CONTRACT_COLS = (((1,), (1,)), ((), ()))


def gelu_value(v):
    return v * 0.5 * (1.0 + lax.erf(v / math.sqrt(2.0)))


def gelu_slope(v):
    return 0.5 * (1.0 + lax.erf(v / math.sqrt(2.0))) + v * jnp.exp(-0.5 * v * v) / math.sqrt(
        2.0 * math.pi
    )


def swap(a):
    return lax.ppermute(a, "row", SWAP)


def gather_tokens(a, core):
    half = a.shape[0] // 2
    mine = lax.dynamic_slice_in_dim(a, core * half, half, 0)
    others = swap(lax.dynamic_slice_in_dim(a, (1 - core) * half, half, 0))
    block = jnp.concatenate([mine, others], axis=1)
    every = lax.all_to_all(jnp.broadcast_to(block[None], (COLS,) + block.shape), "col", 0, 0)
    return every.reshape(COLS * half, block.shape[1])


def scatter_tokens(a, core):
    half = a.shape[0] // COLS
    width = a.shape[1] // 2
    parts = lax.all_to_all(a.reshape(COLS, half, a.shape[1]), "col", 0, 0)
    total = jnp.sum(parts.astype(F32), axis=0).astype(BF)
    others = swap(total[:, width:])
    mine = total[:, :width]
    first = core == 0
    return jnp.concatenate([jnp.where(first, mine, others), jnp.where(first, others, mine)], axis=0)


def scatter_rows(a):
    return lax.psum_scatter(
        a, "row", scatter_dimension=0, axis_index_groups=SAME_CORE, tiled=True
    ).astype(F32)


def gather_rows(a):
    return lax.all_gather(a, "row", axis=0, axis_index_groups=SAME_CORE, tiled=True)


def on_device(tokens, w_in, w_out, cotangent):
    core = lax.rem(lax.axis_index("row"), 2)
    width = w_in.shape[0]
    x_all = gather_tokens(tokens, core)
    w_in2 = jnp.concatenate([w_in, swap(w_in)], axis=0)
    pre = scatter_rows(jnp.dot(x_all, w_in2, preferred_element_type=F32).astype(BF))
    dy_all = gather_tokens(cotangent, core)
    w_out2 = jnp.concatenate([w_out, swap(w_out)], axis=1)
    grad_hidden = scatter_rows(
        lax.dot_general(dy_all, w_out2, CONTRACT_COLS, preferred_element_type=F32).astype(BF)
    )
    hidden = gelu_value(pre).astype(BF)
    h_all = gather_rows(hidden)
    mixed = scatter_tokens(jnp.dot(h_all, w_out2, preferred_element_type=F32).astype(BF), core)
    grad_pre = (grad_hidden * gelu_slope(pre)).astype(BF)
    dg_all = gather_rows(grad_pre)
    grad_tokens = scatter_tokens(
        lax.dot_general(dg_all, w_in2, CONTRACT_COLS, preferred_element_type=F32).astype(BF), core
    )
    factor = 1.0 / math.sqrt(COLS * tokens.shape[0])
    half_in = lax.dot_general(x_all, dg_all, CONTRACT_ROWS, preferred_element_type=F32)
    grad_w_in = (half_in[:width] + swap(half_in[width:].astype(BF)).astype(F32)) * factor
    half_out = lax.dot_general(h_all, dy_all, CONTRACT_ROWS, preferred_element_type=F32)
    grad_w_out = (half_out[:, :width] + swap(half_out[:, width:].astype(BF)).astype(F32)) * factor
    return (mixed, grad_tokens, grad_w_in, grad_w_out)


def solution(mesh):
    placed = (P("col", "row"), P("row", "col"), P("col", "row"), P("col", "row"))
    return jax.shard_map(
        on_device,
        mesh=mesh,
        in_specs=placed,
        out_specs=(P("col", "row"), P("col", "row"), P("row", "col"), P("col", "row")),
        check_vma=False,
    )
```

```python
import math

import jax
import jax.numpy as jnp
from jax import lax
from jax.sharding import PartitionSpec as P

BF = jnp.bfloat16
F32 = jnp.float32
ROWS, COLS = 16, 16
ZS = ROWS // 2
FAR = ZS // 2
SWAP = [(r, r ^ 1) for r in range(ROWS)]
UP = [(2 * z + k, 2 * ((z + 1) % ZS) + k) for z in range(ZS) for k in range(2)]
DOWN = [(b, a) for a, b in UP]
CONTRACT_ROWS = (((0,), (0,)), ((), ()))
CONTRACT_COLS = (((1,), (1,)), ((), ()))
PLAIN = (((1,), (0,)), ((), ()))
PAIRS = [(FAR, 0)] + [(j, ZS - j) for j in range(FAR - 1, 0, -1)]
ORDER = [j for pair in PAIRS for j in pair]


def gelu_value(v):
    return v * 0.5 * (1.0 + lax.erf(v / math.sqrt(2.0)))


def gelu_slope(v):
    return 0.5 * (1.0 + lax.erf(v / math.sqrt(2.0))) + v * jnp.exp(-0.5 * v * v) / math.sqrt(
        2.0 * math.pi
    )


def permute(a, pairs):
    return lax.ppermute(a, "row", pairs)


def product(a, b, dims):
    return lax.dot_general(a, b, dims, preferred_element_type=F32).astype(BF)


def plus(a, b):
    return (a.astype(F32) + b.astype(F32)).astype(BF)


def gather_tokens(a, core):
    half = a.shape[0] // 2
    mine = lax.dynamic_slice_in_dim(a, core * half, half, 0)
    others = permute(lax.dynamic_slice_in_dim(a, (1 - core) * half, half, 0), SWAP)
    block = jnp.concatenate([mine, others], axis=1)
    return lax.all_to_all(jnp.broadcast_to(block[None], (COLS,) + block.shape), "col", 0, 0)


def scatter_tokens(a, core):
    width = a.shape[2] // 2
    parts = lax.all_to_all(a, "col", 0, 0)
    total = jnp.sum(parts.astype(F32), axis=0).astype(BF)
    others = permute(total[:, width:], SWAP)
    mine = total[:, :width]
    first = core == 0
    return jnp.concatenate([jnp.where(first, mine, others), jnp.where(first, others, mine)], axis=0)


def owned_blocks(a, z):
    per = COLS // ZS
    rows = per * a.shape[1]

    def block(j):
        at = lax.rem(z + j, ZS) * per
        return lax.dynamic_slice_in_dim(a, at, per, 0).reshape(rows, a.shape[2])

    return {p: jnp.concatenate([block(p[0]), block(p[1])], axis=0) for p in PAIRS}


def scatter_rows(blocks, weight, dims):
    part = {}
    for pair in PAIRS:
        both = lax.optimization_barrier(product(blocks[pair], weight, dims))
        rows = both.shape[0] // 2
        part[pair[0]], part[pair[1]] = both[:rows], both[rows:]
    half = rows // 2
    up = permute(part[FAR][:half], UP)
    down = permute(part[FAR][half:], DOWN)
    a, b = part[FAR - 1], part[FAR + 1]
    up = permute(jnp.concatenate([plus(a[:half], up), a[half:]], axis=0), UP)
    down = permute(jnp.concatenate([b[:half], plus(b[half:], down)], axis=0), DOWN)
    for j in range(FAR - 2, 0, -1):
        up = permute(plus(part[j], up), UP)
        down = permute(plus(part[ZS - j], down), DOWN)
    return part[0].astype(F32) + up.astype(F32) + down.astype(F32)


def gather_rows(own):
    half = own.shape[0] // 2
    block = {0: own}
    up = down = own
    for j in range(1, FAR):
        up, down = permute(up, UP), permute(down, DOWN)
        block[ZS - j], block[j] = up, down
    up, down = permute(up[:half], UP), permute(down[half:], DOWN)
    block[FAR] = jnp.concatenate([up, down], axis=0)
    return block


def by_column(block, weight, dims, z, half):
    per = COLS // ZS
    groups = [(0,)] + [(j, ZS - j) for j in range(1, FAR)] + [(FAR,)]
    out = jnp.zeros((COLS, half, weight.shape[dims[0][1][0] ^ 1]), BF)
    for group in groups:
        rows = [block[j] for j in group]
        part = lax.optimization_barrier(
            product(rows[0] if len(rows) == 1 else jnp.concatenate(rows, axis=0), weight, dims)
        )
        part = part.reshape(len(group), per, half, part.shape[1])
        for i, j in enumerate(group):
            out = lax.dynamic_update_slice_in_dim(out, part[i], lax.rem(z + j, ZS) * per, 0)
    return out


def on_device(tokens, w_in, w_out, cotangent):
    row = lax.axis_index("row")
    core, z = lax.rem(row, 2), lax.div(row, 2)
    width = w_in.shape[0]
    half = tokens.shape[0] // 2

    x = owned_blocks(gather_tokens(tokens, core), z)
    w_in2 = jnp.concatenate([w_in, permute(w_in, SWAP)], axis=0)
    pre = scatter_rows(x, w_in2, PLAIN)
    hidden, slope = lax.optimization_barrier((gelu_value(pre).astype(BF), gelu_slope(pre)))

    dy = owned_blocks(gather_tokens(cotangent, core), z)
    w_out2 = jnp.concatenate([w_out, permute(w_out, SWAP)], axis=1)
    grad_hidden = scatter_rows(dy, w_out2, CONTRACT_COLS)
    grad_pre = lax.optimization_barrier((grad_hidden * slope).astype(BF))

    h = gather_rows(hidden)
    mixed = scatter_tokens(by_column(h, w_out2, PLAIN, z, half), core)
    dg = gather_rows(grad_pre)
    grad_tokens = scatter_tokens(by_column(dg, w_in2, CONTRACT_COLS, z, half), core)

    def ordered(block):
        return jnp.concatenate([block[j] for j in ORDER], axis=0)

    def paired(blocks):
        return jnp.concatenate([blocks[p] for p in PAIRS], axis=0)

    factor = 1.0 / math.sqrt(COLS * tokens.shape[0])
    half_out = lax.dot_general(ordered(h), paired(dy), CONTRACT_ROWS, preferred_element_type=F32)
    grad_w_out = (
        half_out[:, :width] + permute(half_out[:, width:].astype(BF), SWAP).astype(F32)
    ) * factor
    half_in = lax.dot_general(paired(x), ordered(dg), CONTRACT_ROWS, preferred_element_type=F32)
    grad_w_in = (half_in[:width] + permute(half_in[width:].astype(BF), SWAP).astype(F32)) * factor
    return (mixed, grad_tokens, grad_w_in, grad_w_out)


def solution(mesh):
    placed = (P("col", "row"), P("row", "col"), P("col", "row"), P("col", "row"))
    return jax.shard_map(
        on_device,
        mesh=mesh,
        in_specs=placed,
        out_specs=(P("col", "row"), P("col", "row"), P("row", "col"), P("col", "row")),
        check_vma=False,
    )
```

```python
import math

import jax
import jax.numpy as jnp
from jax import lax
from jax.experimental import pallas as pl
from jax.sharding import PartitionSpec as P

BF = jnp.bfloat16
F32 = jnp.float32
ROWS, COLS = 16, 16
ZS = ROWS // 2
FAR = ZS // 2
SWAP = [(r, r ^ 1) for r in range(ROWS)]
UP = [(2 * z + k, 2 * ((z + 1) % ZS) + k) for z in range(ZS) for k in range(2)]
DOWN = [(b, a) for a, b in UP]
CONTRACT_ROWS = (((0,), (0,)), ((), ()))
CONTRACT_COLS = (((1,), (1,)), ((), ()))
PLAIN = (((1,), (0,)), ((), ()))
SIDE = 4
GROUPS = [(FAR,)] + [(j, ZS - j) for j in range(FAR - 1, 0, -1)] + [(0,)]
ORDER = [j for group in GROUPS for j in group]


def shifted(col, q):
    x, y = col // SIDE + q // SIDE, col % SIDE + q % SIDE
    return (x % SIDE) * SIDE + y % SIDE


def place(z, j, i):
    return 2 * ((z + j) % ZS) + i


def column_shift(j, i):
    return [
        (r * COLS + shifted(c, place(r // 2, j, i)), r * COLS + c)
        for r in range(ROWS)
        for c in range(COLS)
    ]


def gelu_value(v):
    return v * 0.5 * (1.0 + lax.erf(v / math.sqrt(2.0)))


def gelu_slope(v):
    return 0.5 * (1.0 + lax.erf(v / math.sqrt(2.0))) + v * jnp.exp(-0.5 * v * v) / math.sqrt(
        2.0 * math.pi
    )


def permute(a, pairs):
    return lax.ppermute(a, "row", pairs)


def product(a, b, dims):
    return lax.dot_general(a, b, dims, preferred_element_type=F32).astype(BF)


def plus(a, b):
    return (a.astype(F32) + b.astype(F32)).astype(BF)


def after(a, other):
    anywhere = pl.BlockSpec(memory_space=pl.ANY)
    return pl.pallas_call(
        lambda a_ref, other_ref, out_ref: None,
        out_shape=jax.ShapeDtypeStruct(a.shape, a.dtype),
        in_specs=[anywhere, anywhere],
        out_specs=anywhere,
        input_output_aliases={0: 0},
    )(a, other)


def token_half(a, core):
    half = a.shape[0] // 2
    mine = lax.dynamic_slice_in_dim(a, core * half, half, 0)
    others = permute(lax.dynamic_slice_in_dim(a, (1 - core) * half, half, 0), SWAP)
    return jnp.concatenate([mine, others], axis=1)


def token_whole(total, core):
    width = total.shape[1] // 2
    total = total.astype(BF)
    others = permute(total[:, width:], SWAP)
    mine = total[:, :width]
    first = core == 0
    return jnp.concatenate([jnp.where(first, mine, others), jnp.where(first, others, mine)], axis=0)


def blocks_by_permute(block):
    return {
        j: jnp.concatenate(
            [lax.ppermute(block, ("row", "col"), column_shift(j, i)) for i in range(2)], axis=0
        )
        for j in ORDER
    }


def gather_columns(block):
    return lax.all_to_all(jnp.broadcast_to(block[None], (COLS,) + block.shape), "col", 0, 0)


def blocks_of(every, z, col):
    return {
        j: jnp.concatenate(
            [
                lax.dynamic_index_in_dim(every, shifted(col, place(z, j, i)), 0, keepdims=False)
                for i in range(2)
            ],
            axis=0,
        )
        for j in ORDER
    }


def scatter_rows(blocks, weight, dims):
    part = {}
    for group in GROUPS:
        together = [blocks[j] for j in group]
        together = together[0] if len(group) == 1 else jnp.concatenate(together, axis=0)
        made = lax.optimization_barrier(product(together, weight, dims))
        rows = made.shape[0] // len(group)
        for n, j in enumerate(group):
            part[j] = made[n * rows : (n + 1) * rows]
    half = rows // 2
    up = permute(part[FAR][:half], UP)
    down = permute(part[FAR][half:], DOWN)
    a, b = part[FAR - 1], part[FAR + 1]
    up = permute(jnp.concatenate([plus(a[:half], up), a[half:]], axis=0), UP)
    down = permute(jnp.concatenate([b[:half], plus(b[half:], down)], axis=0), DOWN)
    for j in range(FAR - 2, 0, -1):
        mark = up
        up = permute(plus(part[j], up), UP)
        down = permute(plus(part[ZS - j], down), DOWN)
    return part[0].astype(F32) + up.astype(F32) + down.astype(F32), mark


def gather_rows(own):
    half = own.shape[0] // 2
    block = {0: own}
    up = down = own
    for j in range(1, FAR):
        up, down = permute(up, UP), permute(down, DOWN)
        block[ZS - j], block[j] = up, down
    up, down = permute(up[:half], UP), permute(down[half:], DOWN)
    block[FAR] = jnp.concatenate([up, down], axis=0)
    return block


def products(block, weight, dims):
    part = {}
    for group in reversed(GROUPS):
        rows = [block[j] for j in group]
        made = product(rows[0] if len(rows) == 1 else jnp.concatenate(rows, axis=0), weight, dims)
        made = lax.optimization_barrier(made)
        each = made.shape[0] // len(group)
        for n, j in enumerate(group):
            part[j] = made[n * each : (n + 1) * each]
    return part


def sum_by_all_to_all(part, z, col):
    half = part[0].shape[0] // 2
    out = jnp.zeros((COLS, half, part[0].shape[1]), BF)
    for j in ORDER:
        for i in range(2):
            piece = part[j][i * half : (i + 1) * half]
            out = lax.dynamic_update_index_in_dim(out, piece, shifted(col, place(z, j, i)), 0)
    return jnp.sum(lax.all_to_all(out, "col", 0, 0).astype(F32), axis=0)


def sum_by_permute(part):
    half = part[0].shape[0] // 2
    total = 0.0
    for j in reversed(ORDER):
        for i in range(2):
            back = [(b, a) for a, b in column_shift(j, i)]
            piece = lax.ppermute(part[j][i * half : (i + 1) * half], ("row", "col"), back)
            total = total + piece.astype(F32)
    return total


def on_device(tokens, w_in, w_out, cotangent):
    row, col = lax.axis_index("row"), lax.axis_index("col")
    core, z = lax.rem(row, 2), lax.div(row, 2)
    width = w_in.shape[0]

    x = blocks_by_permute(token_half(tokens, core))
    w_in2 = jnp.concatenate([w_in, permute(w_in, SWAP)], axis=0)
    pre, mark = scatter_rows(x, w_in2, PLAIN)
    hidden, slope = lax.optimization_barrier((gelu_value(pre).astype(BF), gelu_slope(pre)))

    dy = blocks_of(after(gather_columns(token_half(cotangent, core)), mark), z, col)
    w_out2 = jnp.concatenate([w_out, permute(w_out, SWAP)], axis=1)
    grad_hidden, _ = scatter_rows(dy, w_out2, CONTRACT_COLS)
    grad_pre = lax.optimization_barrier((grad_hidden * slope).astype(BF))

    h = gather_rows(hidden)
    mixed = token_whole(sum_by_all_to_all(products(h, w_out2, PLAIN), z, col), core)
    dg = gather_rows(grad_pre)
    grad_tokens = token_whole(sum_by_permute(products(dg, w_in2, CONTRACT_COLS)), core)

    def ordered(block):
        return jnp.concatenate([block[j] for j in ORDER], axis=0)

    factor = 1.0 / math.sqrt(COLS * tokens.shape[0])
    half_out = lax.dot_general(ordered(h), ordered(dy), CONTRACT_ROWS, preferred_element_type=F32)
    grad_w_out = (
        half_out[:, :width] + permute(half_out[:, width:].astype(BF), SWAP).astype(F32)
    ) * factor
    half_in = lax.dot_general(ordered(x), ordered(dg), CONTRACT_ROWS, preferred_element_type=F32)
    grad_w_in = (half_in[:width] + permute(half_in[width:].astype(BF), SWAP).astype(F32)) * factor
    return (mixed, grad_tokens, grad_w_in, grad_w_out)


def solution(mesh):
    placed = (P("col", "row"), P("row", "col"), P("col", "row"), P("col", "row"))
    return jax.shard_map(
        on_device,
        mesh=mesh,
        in_specs=placed,
        out_specs=(P("col", "row"), P("col", "row"), P("row", "col"), P("col", "row")),
        check_vma=False,
    )
```

```python
import math

import jax
import jax.numpy as jnp
from jax import lax
from jax.experimental import pallas as pl
from jax.sharding import PartitionSpec as P

BF = jnp.bfloat16
F32 = jnp.float32
ROWS, COLS = 16, 16
ZS = ROWS // 2
FAR = ZS // 2
SWAP = [(r, r ^ 1) for r in range(ROWS)]
UP = [(2 * z + k, 2 * ((z + 1) % ZS) + k) for z in range(ZS) for k in range(2)]
DOWN = [(b, a) for a, b in UP]
CONTRACT_ROWS = (((0,), (0,)), ((), ()))
CONTRACT_COLS = (((1,), (1,)), ((), ()))
PLAIN = (((1,), (0,)), ((), ()))
PAIRS = [(FAR, 0)] + [(j, ZS - j) for j in range(FAR - 1, 0, -1)]
ORDER = [j for pair in PAIRS for j in pair]


def gelu_value(v):
    return v * 0.5 * (1.0 + lax.erf(v / math.sqrt(2.0)))


def gelu_slope(v):
    return 0.5 * (1.0 + lax.erf(v / math.sqrt(2.0))) + v * jnp.exp(-0.5 * v * v) / math.sqrt(
        2.0 * math.pi
    )


def permute(a, pairs):
    return lax.ppermute(a, "row", pairs)


def product(a, b, dims):
    return lax.dot_general(a, b, dims, preferred_element_type=F32).astype(BF)


def plus(a, b):
    return (a.astype(F32) + b.astype(F32)).astype(BF)


def after(a, other):
    anywhere = pl.BlockSpec(memory_space=pl.ANY)
    return pl.pallas_call(
        lambda a_ref, other_ref, out_ref: None,
        out_shape=jax.ShapeDtypeStruct(a.shape, a.dtype),
        in_specs=[anywhere, anywhere],
        out_specs=anywhere,
        input_output_aliases={0: 0},
    )(a, other)


def token_half(a, core):
    half = a.shape[0] // 2
    mine = lax.dynamic_slice_in_dim(a, core * half, half, 0)
    others = permute(lax.dynamic_slice_in_dim(a, (1 - core) * half, half, 0), SWAP)
    return jnp.concatenate([mine, others], axis=1)


def gather_columns(block):
    return lax.all_to_all(jnp.broadcast_to(block[None], (COLS,) + block.shape), "col", 0, 0)


def scatter_tokens(a, core):
    width = a.shape[2] // 2
    parts = lax.all_to_all(a, "col", 0, 0)
    total = jnp.sum(parts.astype(F32), axis=0).astype(BF)
    others = permute(total[:, width:], SWAP)
    mine = total[:, :width]
    first = core == 0
    return jnp.concatenate([jnp.where(first, mine, others), jnp.where(first, others, mine)], axis=0)


def owned_blocks(a, z):
    per = COLS // ZS
    rows = per * a.shape[1]

    def block(j):
        at = lax.rem(z + j, ZS) * per
        return lax.dynamic_slice_in_dim(a, at, per, 0).reshape(rows, a.shape[2])

    return {p: jnp.concatenate([block(p[0]), block(p[1])], axis=0) for p in PAIRS}


def scatter_rows(blocks, weight, dims):
    part = {}
    for pair in PAIRS:
        both = lax.optimization_barrier(product(blocks[pair], weight, dims))
        rows = both.shape[0] // 2
        part[pair[0]], part[pair[1]] = both[:rows], both[rows:]
    half = rows // 2
    up = permute(part[FAR][:half], UP)
    down = permute(part[FAR][half:], DOWN)
    a, b = part[FAR - 1], part[FAR + 1]
    up = permute(jnp.concatenate([plus(a[:half], up), a[half:]], axis=0), UP)
    down = permute(jnp.concatenate([b[:half], plus(b[half:], down)], axis=0), DOWN)
    for j in range(FAR - 2, 0, -1):
        mark = up
        up = permute(plus(part[j], up), UP)
        down = permute(plus(part[ZS - j], down), DOWN)
    return part[0].astype(F32) + up.astype(F32) + down.astype(F32), mark


def gather_rows(own):
    half = own.shape[0] // 2
    block = {0: own}
    up = down = own
    for j in range(1, FAR):
        up, down = permute(up, UP), permute(down, DOWN)
        block[ZS - j], block[j] = up, down
    up, down = permute(up[:half], UP), permute(down[half:], DOWN)
    block[FAR] = jnp.concatenate([up, down], axis=0)
    return block


def by_column(block, weight, dims, z, half):
    per = COLS // ZS
    groups = [(0,)] + [(j, ZS - j) for j in range(1, FAR)] + [(FAR,)]
    out = jnp.zeros((COLS, half, weight.shape[dims[0][1][0] ^ 1]), BF)
    for group in groups:
        rows = [block[j] for j in group]
        part = lax.optimization_barrier(
            product(rows[0] if len(rows) == 1 else jnp.concatenate(rows, axis=0), weight, dims)
        )
        part = part.reshape(len(group), per, half, part.shape[1])
        for i, j in enumerate(group):
            out = lax.dynamic_update_slice_in_dim(out, part[i], lax.rem(z + j, ZS) * per, 0)
    return out


def interleave(parts, per):
    parts = [p.reshape(per, p.shape[0] // per, p.shape[1]) for p in parts]
    whole = jnp.concatenate(parts, axis=1)
    return whole.reshape(per * whole.shape[1], whole.shape[2])


def on_device(tokens, w_in, w_out, cotangent):
    row = lax.axis_index("row")
    core, z = lax.rem(row, 2), lax.div(row, 2)
    width = w_in.shape[0]
    half = tokens.shape[0] // 2
    part = half // 2
    per = COLS // ZS

    mine = token_half(tokens, core)
    x = [owned_blocks(gather_columns(mine[n * part : (n + 1) * part]), z) for n in range(2)]
    w_in2 = jnp.concatenate([w_in, permute(w_in, SWAP)], axis=0)
    pre, marks = zip(*(scatter_rows(blocks, w_in2, PLAIN) for blocks in x))
    pre = interleave(pre, per)
    hidden, slope = lax.optimization_barrier((gelu_value(pre).astype(BF), gelu_slope(pre)))

    dy = owned_blocks(after(gather_columns(token_half(cotangent, core)), marks[1]), z)
    w_out2 = jnp.concatenate([w_out, permute(w_out, SWAP)], axis=1)
    grad_hidden, _ = scatter_rows(dy, w_out2, CONTRACT_COLS)
    grad_pre = lax.optimization_barrier((grad_hidden * slope).astype(BF))

    def ordered(block):
        return jnp.concatenate([block[j] for j in ORDER], axis=0)

    factor = 1.0 / math.sqrt(COLS * tokens.shape[0])

    h = gather_rows(hidden)
    mixed = scatter_tokens(by_column(h, w_out2, PLAIN, z, half), core)
    dy_all = jnp.concatenate([dy[p] for p in PAIRS], axis=0)
    half_out = lax.dot_general(ordered(h), dy_all, CONTRACT_ROWS, preferred_element_type=F32)
    sent_out = half_out[:, width:].astype(BF)
    grad_w_out = (half_out[:, :width] + permute(sent_out, SWAP).astype(F32)) * factor

    dg = gather_rows(grad_pre)
    dg[FAR] = after(dg[FAR], sent_out)
    last = by_column(dg, w_in2, CONTRACT_COLS, z, half)
    grad_tokens = scatter_tokens(last, core)
    x_all = jnp.concatenate(
        [interleave([x[0][p], x[1][p]], 2 * per) for p in PAIRS], axis=0
    )
    dg_all = after(ordered(dg), last)
    half_in = lax.dot_general(x_all, dg_all, CONTRACT_ROWS, preferred_element_type=F32)
    grad_w_in = (half_in[:width] + permute(half_in[width:].astype(BF), SWAP).astype(F32)) * factor
    return (mixed, grad_tokens, grad_w_in, grad_w_out)


def solution(mesh):
    placed = (P("col", "row"), P("row", "col"), P("col", "row"), P("col", "row"))
    return jax.shard_map(
        on_device,
        mesh=mesh,
        in_specs=placed,
        out_specs=(P("col", "row"), P("col", "row"), P("row", "col"), P("col", "row")),
        check_vma=False,
    )
```

```python
import math

import jax
import jax.numpy as jnp
from jax import lax
from jax.experimental import pallas as pl
from jax.experimental.pallas import tpu as pltpu
from jax.sharding import PartitionSpec as P

BF = jnp.bfloat16
F32 = jnp.float32
ROWS, COLS = 16, 16
ZS = ROWS // 2
FAR = ZS // 2
SWAP = [(r, r ^ 1) for r in range(ROWS)]
UP = [(2 * z + k, 2 * ((z + 1) % ZS) + k) for z in range(ZS) for k in range(2)]
DOWN = [(b, a) for a, b in UP]
CONTRACT_ROWS = (((0,), (0,)), ((), ()))
CONTRACT_COLS = (((1,), (1,)), ((), ()))
PLAIN = (((1,), (0,)), ((), ()))
PAIRS = [(FAR, 0)] + [(j, ZS - j) for j in range(FAR - 1, 0, -1)]
ORDER = [j for pair in PAIRS for j in pair]


def gelu_value(v):
    return v * 0.5 * (1.0 + lax.erf(v / math.sqrt(2.0)))


def gelu_slope(v):
    return 0.5 * (1.0 + lax.erf(v / math.sqrt(2.0))) + v * jnp.exp(-0.5 * v * v) / math.sqrt(
        2.0 * math.pi
    )


def permute(a, pairs):
    return lax.ppermute(a, "row", pairs)


def product(a, b, dims):
    return lax.dot_general(a, b, dims, preferred_element_type=F32).astype(BF)


def plus(a, b):
    return (a.astype(F32) + b.astype(F32)).astype(BF)


def after(a, other):
    anywhere = pl.BlockSpec(memory_space=pl.ANY)
    return pl.pallas_call(
        lambda a_ref, other_ref, out_ref: None,
        out_shape=jax.ShapeDtypeStruct(a.shape, a.dtype),
        in_specs=[anywhere, anywhere],
        out_specs=anywhere,
        input_output_aliases={0: 0},
    )(a, other)


def token_half(a, core):
    half = a.shape[0] // 2
    mine = lax.dynamic_slice_in_dim(a, core * half, half, 0)
    others = permute(lax.dynamic_slice_in_dim(a, (1 - core) * half, half, 0), SWAP)
    return jnp.concatenate([mine, others], axis=1)


def for_columns(block):
    return jnp.broadcast_to(block[None], (COLS,) + block.shape)


def gather_columns(copies):
    return lax.all_to_all(copies, "col", 0, 0)


def sum_columns(a):
    return jnp.sum(lax.all_to_all(a, "col", 0, 0).astype(F32), axis=0).astype(BF)


def token_whole(total, core):
    width = total.shape[1] // 2
    others = permute(total[:, width:], SWAP)
    mine = total[:, :width]
    first = core == 0
    return jnp.concatenate([jnp.where(first, mine, others), jnp.where(first, others, mine)], axis=0)


def owned_blocks(a, z):
    per = COLS // ZS
    rows = per * a.shape[1]

    def block(j):
        at = lax.rem(z + j, ZS) * per
        return lax.dynamic_slice_in_dim(a, at, per, 0).reshape(rows, a.shape[2])

    return {p: jnp.concatenate([block(p[0]), block(p[1])], axis=0) for p in PAIRS}


def scatter_rows(blocks, weight, dims):
    part = {}
    for pair in PAIRS:
        both = lax.optimization_barrier(product(blocks[pair], weight, dims))
        if pair == PAIRS[1]:
            made = both
        rows = both.shape[0] // 2
        part[pair[0]], part[pair[1]] = both[:rows], both[rows:]
    half = rows // 2
    up = permute(part[FAR][:half], UP)
    down = permute(part[FAR][half:], DOWN)
    a, b = part[FAR - 1], part[FAR + 1]
    up = permute(jnp.concatenate([plus(a[:half], up), a[half:]], axis=0), UP)
    down = permute(jnp.concatenate([b[:half], plus(b[half:], down)], axis=0), DOWN)
    for j in range(FAR - 2, 0, -1):
        mark = up
        up = permute(plus(part[j], up), UP)
        down = permute(plus(part[ZS - j], down), DOWN)
    return part[0].astype(F32) + up.astype(F32) + down.astype(F32), made, mark


def gather_rows(own):
    half = own.shape[0] // 2
    pieces = [(own, 0, 0)]
    up = down = own
    for j in range(1, FAR):
        up, down = permute(up, UP), permute(down, DOWN)
        pieces += [(up, ZS - j, 0), (down, j, 0)]
    return pieces + [(permute(up[:half], UP), FAR, 0), (permute(down[half:], DOWN), FAR, half)]


def join_and_multiply(pieces, weight, dims, z, first=None):
    block, inner = pieces[0][0].shape
    rows = ZS * block
    outer = weight.shape[dims[0][1][0] ^ 1]
    step = 2 * block

    def kernel(z_ref, *refs):
        piece_refs, weight_ref = refs[: len(pieces)], refs[len(pieces)]
        joined_ref, made_ref = refs[-2:]
        for ref, (piece, j, first) in zip(piece_refs, pieces):
            at = lax.rem(z_ref[0] + j, ZS) * block + first
            count = piece.shape[0]
            joined_ref[pl.ds(pl.multiple_of(at, count), count), :] = ref[...]

        @pl.loop(0, rows // step)
        def _(n):
            these = pl.ds(pl.multiple_of(n * step, step), step)
            made_ref[these, :] = lax.dot_general(
                joined_ref[these, :], weight_ref[...], dims, preferred_element_type=F32
            ).astype(BF)

    vmem = pl.BlockSpec(memory_space=pltpu.VMEM)
    return pl.pallas_call(
        kernel,
        out_shape=(
            jax.ShapeDtypeStruct((rows, inner), BF),
            jax.ShapeDtypeStruct((rows, outer), BF),
        ),
        in_specs=[pl.BlockSpec(memory_space=pltpu.SMEM)] + [vmem] * (len(pieces) + 1)
        + ([] if first is None else [pl.BlockSpec(memory_space=pl.ANY)]),
        out_specs=(vmem, vmem),
        compiler_params=pltpu.CompilerParams(vmem_limit_bytes=40 * 2**20),
        cost_estimate=pl.CostEstimate(
            flops=2 * rows * inner * outer,
            bytes_accessed=2 * (2 * rows * inner + inner * outer + rows * outer),
            transcendentals=0,
        ),
    )(z.reshape(1), *(piece for piece, _, _ in pieces), weight, *([] if first is None else [first]))


def add_halves(mine, others, factor):
    steps = 4
    rows, columns = others.shape[0] // steps, others.shape[1]
    spec = pl.BlockSpec((rows, columns), lambda n: (n, 0))

    def kernel(mine_ref, others_ref, out_ref):
        out_ref[...] = (mine_ref[...] + others_ref[...].astype(F32)) * factor

    return pl.pallas_call(
        kernel,
        out_shape=jax.ShapeDtypeStruct(others.shape, F32),
        grid=(steps,),
        in_specs=[spec, spec],
        out_specs=spec,
        cost_estimate=pl.CostEstimate(flops=0, bytes_accessed=0, transcendentals=0),
    )(mine, others)


def on_device(tokens, w_in, w_out, cotangent):
    row = lax.axis_index("row")
    core, z = lax.rem(row, 2), lax.div(row, 2)
    width = w_in.shape[0]
    half = tokens.shape[0] // 2

    def by_column(a):
        return a.reshape(COLS, half, a.shape[1])

    def by_token(a):
        return a.reshape(COLS * half, a.shape[2])

    x_all = gather_columns(for_columns(token_half(tokens, core)))
    dy_sent = after(for_columns(token_half(cotangent, core)), w_in)
    w_in2 = jnp.concatenate([w_in, permute(w_in, SWAP)], axis=0)
    w_out2 = jnp.concatenate([w_out, permute(w_out, SWAP)], axis=1)
    w_out2_t = after(w_out2.T, w_in2)
    x_all = after(after(x_all, w_out2_t), dy_sent)
    pre, made, mark = scatter_rows(owned_blocks(x_all, z), w_in2, PLAIN)
    hidden, slope = lax.optimization_barrier((gelu_value(pre).astype(BF), gelu_slope(pre)))

    dy_all = after(gather_columns(after(dy_sent, made)), mark)
    grad_hidden, _, _ = scatter_rows(owned_blocks(dy_all, z), w_out2, CONTRACT_COLS)
    grad_pre = lax.optimization_barrier((grad_hidden * slope).astype(BF))

    h_all, made = join_and_multiply(gather_rows(hidden), w_out2, PLAIN, z)
    total = sum_columns(by_column(made))
    mixed = token_whole(total, core)
    dg_all, made = join_and_multiply(gather_rows(grad_pre), w_in2, CONTRACT_COLS, z)
    total = sum_columns(by_column(made))

    factor = 1.0 / math.sqrt(COLS * tokens.shape[0])
    half_in = lax.dot_general(by_token(x_all), dg_all, CONTRACT_ROWS, preferred_element_type=F32)
    grad_w_in = add_halves(half_in, permute(half_in[width:].astype(BF), SWAP), factor)
    half_out = lax.dot_general(
        after(h_all, made), by_token(dy_all), CONTRACT_ROWS, preferred_element_type=F32
    )
    grad_w_out = add_halves(half_out, permute(half_out[:, width:].astype(BF), SWAP), factor)
    grad_tokens = token_whole(after(after(total, grad_w_in), grad_w_out), core)
    return (mixed, grad_tokens, grad_w_in, grad_w_out)


def solution(mesh):
    placed = (P("col", "row"), P("row", "col"), P("col", "row"), P("col", "row"))
    return jax.shard_map(
        on_device,
        mesh=mesh,
        in_specs=placed,
        out_specs=(P("col", "row"), P("col", "row"), P("row", "col"), P("col", "row")),
        check_vma=False,
    )
```

```python
import math

import jax
import jax.numpy as jnp
from jax import lax
from jax.experimental import pallas as pl
from jax.experimental.pallas import tpu as pltpu
from jax.sharding import PartitionSpec as P

BF = jnp.bfloat16
F32 = jnp.float32
ROWS, COLS = 16, 16
ZS = ROWS // 2
FAR = ZS // 2
SWAP = [(r, r ^ 1) for r in range(ROWS)]
UP = [(2 * z + k, 2 * ((z + 1) % ZS) + k) for z in range(ZS) for k in range(2)]
DOWN = [(b, a) for a, b in UP]
CONTRACT_ROWS = (((0,), (0,)), ((), ()))
CONTRACT_COLS = (((1,), (1,)), ((), ()))
PLAIN = (((1,), (0,)), ((), ()))
PAIRS = [(FAR, 0)] + [(j, ZS - j) for j in range(FAR - 1, 0, -1)]
ORDER = [j for pair in PAIRS for j in pair]


def gelu_value(v):
    return v * 0.5 * (1.0 + lax.erf(v / math.sqrt(2.0)))


def gelu_slope(v):
    return 0.5 * (1.0 + lax.erf(v / math.sqrt(2.0))) + v * jnp.exp(-0.5 * v * v) / math.sqrt(
        2.0 * math.pi
    )


def permute(a, pairs):
    return lax.ppermute(a, "row", pairs)


def product(a, b, dims):
    return lax.dot_general(a, b, dims, preferred_element_type=F32).astype(BF)


def plus(a, b):
    return (a.astype(F32) + b.astype(F32)).astype(BF)


def after(a, other):
    anywhere = pl.BlockSpec(memory_space=pl.ANY)
    return pl.pallas_call(
        lambda a_ref, other_ref, out_ref: None,
        out_shape=jax.ShapeDtypeStruct(a.shape, a.dtype),
        in_specs=[anywhere, anywhere],
        out_specs=anywhere,
        input_output_aliases={0: 0},
    )(a, other)


def token_half(a, core):
    half = a.shape[0] // 2
    mine = lax.dynamic_slice_in_dim(a, core * half, half, 0)
    others = permute(lax.dynamic_slice_in_dim(a, (1 - core) * half, half, 0), SWAP)
    return jnp.concatenate([mine, others], axis=1)


def for_columns(block):
    return jnp.broadcast_to(block[None], (COLS,) + block.shape)


def gather_columns(copies):
    return lax.all_to_all(copies, "col", 0, 0)


def sum_columns(a):
    return jnp.sum(lax.all_to_all(a, "col", 0, 0).astype(F32), axis=0).astype(BF)


def token_whole(total, core):
    width = total.shape[1] // 2
    others = permute(total[:, width:], SWAP)
    mine = total[:, :width]
    first = core == 0
    return jnp.concatenate([jnp.where(first, mine, others), jnp.where(first, others, mine)], axis=0)


def owned_blocks(a, z):
    per = COLS // ZS
    rows = per * a.shape[1]

    def block(j):
        at = lax.rem(z + j, ZS) * per
        return lax.dynamic_slice_in_dim(a, at, per, 0).reshape(rows, a.shape[2])

    return {p: jnp.concatenate([block(p[0]), block(p[1])], axis=0) for p in PAIRS}


def scatter_rows(blocks, weight, dims):
    part = {}
    for pair in PAIRS:
        both = lax.optimization_barrier(product(blocks[pair], weight, dims))
        if pair == PAIRS[1]:
            made = both
        rows = both.shape[0] // 2
        part[pair[0]], part[pair[1]] = both[:rows], both[rows:]
    half = rows // 2
    up = permute(part[FAR][:half], UP)
    down = permute(part[FAR][half:], DOWN)
    a, b = part[FAR - 1], part[FAR + 1]
    up = permute(jnp.concatenate([plus(a[:half], up), a[half:]], axis=0), UP)
    down = permute(jnp.concatenate([b[:half], plus(b[half:], down)], axis=0), DOWN)
    for j in range(FAR - 2, 0, -1):
        if j == FAR - 2:
            mark = up
        up = permute(plus(part[j], up), UP)
        down = permute(plus(part[ZS - j], down), DOWN)
    return part[0].astype(F32) + up.astype(F32) + down.astype(F32), made, mark


def gather_rows(own, work=None):
    half = own.shape[0] // 2
    pieces = [(own, 0, 0)]
    up = down = own
    for j in range(1, FAR):
        up, down = permute(up, UP), permute(down, DOWN)
        pieces += [(up, ZS - j, 0), (down, j, 0)]
    last = up[:half]
    if work is not None:
        last = after(last, work(pieces[1][0]))
    return pieces + [(permute(last, UP), FAR, 0), (permute(down[half:], DOWN), FAR, half)]


def join_and_multiply(pieces, weight, dims, z, first=None):
    block, inner = pieces[0][0].shape
    rows = ZS * block
    outer = weight.shape[dims[0][1][0] ^ 1]
    step = 2 * block

    def kernel(z_ref, *refs):
        piece_refs, weight_ref = refs[: len(pieces)], refs[len(pieces)]
        joined_ref, made_ref = refs[-2:]
        for ref, (piece, j, first) in zip(piece_refs, pieces):
            at = lax.rem(z_ref[0] + j, ZS) * block + first
            count = piece.shape[0]
            joined_ref[pl.ds(pl.multiple_of(at, count), count), :] = ref[...]

        @pl.loop(0, rows // step)
        def _(n):
            these = pl.ds(pl.multiple_of(n * step, step), step)
            made_ref[these, :] = lax.dot_general(
                joined_ref[these, :], weight_ref[...], dims, preferred_element_type=F32
            ).astype(BF)

    vmem = pl.BlockSpec(memory_space=pltpu.VMEM)
    return pl.pallas_call(
        kernel,
        out_shape=(
            jax.ShapeDtypeStruct((rows, inner), BF),
            jax.ShapeDtypeStruct((rows, outer), BF),
        ),
        in_specs=[pl.BlockSpec(memory_space=pltpu.SMEM)] + [vmem] * (len(pieces) + 1)
        + ([] if first is None else [pl.BlockSpec(memory_space=pl.ANY)]),
        out_specs=(vmem, vmem),
        compiler_params=pltpu.CompilerParams(vmem_limit_bytes=40 * 2**20),
        cost_estimate=pl.CostEstimate(
            flops=2 * rows * inner * outer,
            bytes_accessed=2 * (2 * rows * inner + inner * outer + rows * outer),
            transcendentals=0,
        ),
    )(z.reshape(1), *(piece for piece, _, _ in pieces), weight, *([] if first is None else [first]))


def weight_gradient(left, right, along, flops=0):
    rows, m = left.shape
    n = right.shape[1]
    steps = 4
    vmem = pl.BlockSpec(memory_space=pltpu.VMEM)
    if along == 0:
        tile = n // steps
        shape = (m // 2, n)
        left_spec, right_spec = vmem, pl.BlockSpec((rows, tile), lambda i: (0, i))
        out_spec = pl.BlockSpec((m // 2, tile), lambda i: (0, i))
    else:
        tile = m // steps
        shape = (m, n // 2)
        left_spec, right_spec = pl.BlockSpec((rows, tile), lambda i: (0, i)), vmem
        out_spec = pl.BlockSpec((tile, n // 2), lambda i: (i, 0))

    def kernel(left_ref, right_ref, mine_ref, others_ref):
        made = lax.dot_general(
            left_ref[...], right_ref[...], CONTRACT_ROWS, preferred_element_type=F32
        )
        if along == 0:
            mine_ref[...] = made[: m // 2]
            others_ref[...] = made[m // 2 :].astype(BF)
        else:
            mine_ref[...] = made[:, : n // 2]
            others_ref[...] = made[:, n // 2 :].astype(BF)

    return pl.pallas_call(
        kernel,
        out_shape=(jax.ShapeDtypeStruct(shape, F32), jax.ShapeDtypeStruct(shape, BF)),
        grid=(steps,),
        in_specs=[left_spec, right_spec],
        out_specs=(out_spec, out_spec),
        compiler_params=pltpu.CompilerParams(vmem_limit_bytes=40 * 2**20),
        cost_estimate=pl.CostEstimate(flops=flops, bytes_accessed=flops // 256, transcendentals=0),
    )(left, right)


def add_halves(mine, others, factor):
    steps = 4
    rows, columns = others.shape[0] // steps, others.shape[1]
    spec = pl.BlockSpec((rows, columns), lambda n: (n, 0))

    def kernel(mine_ref, others_ref, out_ref):
        out_ref[...] = (mine_ref[...] + others_ref[...].astype(F32)) * factor

    return pl.pallas_call(
        kernel,
        out_shape=jax.ShapeDtypeStruct(others.shape, F32),
        grid=(steps,),
        in_specs=[spec, spec],
        out_specs=spec,
        cost_estimate=pl.CostEstimate(flops=0, bytes_accessed=0, transcendentals=0),
    )(mine, others)


def on_device(tokens, w_in, w_out, cotangent):
    row = lax.axis_index("row")
    core, z = lax.rem(row, 2), lax.div(row, 2)
    width = w_in.shape[0]
    half = tokens.shape[0] // 2

    def by_column(a):
        return a.reshape(COLS, half, a.shape[1])

    def by_token(a):
        return a.reshape(COLS * half, a.shape[2])

    x_all = gather_columns(for_columns(token_half(tokens, core)))
    dy_sent = after(for_columns(token_half(cotangent, core)), w_in)
    w_in2 = jnp.concatenate([w_in, permute(w_in, SWAP)], axis=0)
    w_out2 = jnp.concatenate([w_out, permute(w_out, SWAP)], axis=1)
    w_out2_t = after(w_out2.T, w_in2)
    x_all = after(after(x_all, w_out2_t), dy_sent)
    pre, made, mark = scatter_rows(owned_blocks(x_all, z), w_in2, PLAIN)
    hidden, slope = lax.optimization_barrier((gelu_value(pre).astype(BF), gelu_slope(pre)))

    dy_all = after(gather_columns(after(dy_sent, made)), mark)
    grad_hidden, _, _ = scatter_rows(owned_blocks(dy_all, z), w_out2, CONTRACT_COLS)
    grad_pre = lax.optimization_barrier((grad_hidden * slope).astype(BF))

    h_all, made = join_and_multiply(gather_rows(hidden), w_out2, PLAIN, z)
    total = sum_columns(by_column(made))
    mixed = token_whole(total, core)
    w_out_halves = []

    def w_out_gradient(mark):
        flops = 2 * h_all.shape[0] * h_all.shape[1] * x_all.shape[2]
        w_out_halves.extend(weight_gradient(after(h_all, mark), by_token(dy_all), 1, flops))
        return w_out_halves[1]

    pieces = gather_rows(grad_pre, w_out_gradient)
    dg_all, made = join_and_multiply(pieces, w_in2, CONTRACT_COLS, z)
    total = sum_columns(by_column(made))

    factor = 1.0 / math.sqrt(COLS * tokens.shape[0])
    half_in, others_in = weight_gradient(by_token(x_all), dg_all, 0)
    grad_w_in = add_halves(half_in, permute(others_in, SWAP), factor)
    half_out, others_out = w_out_halves
    grad_w_out = add_halves(half_out, permute(others_out, SWAP), factor)
    grad_tokens = token_whole(after(after(total, grad_w_in), grad_w_out), core)
    return (mixed, grad_tokens, grad_w_in, grad_w_out)


def solution(mesh):
    placed = (P("col", "row"), P("row", "col"), P("col", "row"), P("col", "row"))
    return jax.shard_map(
        on_device,
        mesh=mesh,
        in_specs=placed,
        out_specs=(P("col", "row"), P("col", "row"), P("row", "col"), P("col", "row")),
        check_vma=False,
    )
```

```python
import math

import jax
import jax.numpy as jnp
from jax import lax
from jax.experimental import pallas as pl
from jax.experimental.pallas import tpu as pltpu
from jax.sharding import PartitionSpec as P

BF = jnp.bfloat16
F32 = jnp.float32
ROWS, COLS = 16, 16
ZS = ROWS // 2
FAR = ZS // 2
SWAP = [(r, r ^ 1) for r in range(ROWS)]
UP = [(2 * z + k, 2 * ((z + 1) % ZS) + k) for z in range(ZS) for k in range(2)]
DOWN = [(b, a) for a, b in UP]
CONTRACT_ROWS = (((0,), (0,)), ((), ()))
CONTRACT_COLS = (((1,), (1,)), ((), ()))
PLAIN = (((1,), (0,)), ((), ()))
PAIRS = [(FAR, 0)] + [(j, ZS - j) for j in range(FAR - 1, 0, -1)]
ORDER = [j for pair in PAIRS for j in pair]


def gelu_value(v):
    return v * 0.5 * (1.0 + lax.erf(v / math.sqrt(2.0)))


def gelu_slope(v):
    return 0.5 * (1.0 + lax.erf(v / math.sqrt(2.0))) + v * jnp.exp(-0.5 * v * v) / math.sqrt(
        2.0 * math.pi
    )


def permute(a, pairs):
    return lax.ppermute(a, "row", pairs)


def product(a, b, dims):
    return lax.dot_general(a, b, dims, preferred_element_type=F32).astype(BF)


def plus(a, b):
    return (a.astype(F32) + b.astype(F32)).astype(BF)


def after(a, other):
    anywhere = pl.BlockSpec(memory_space=pl.ANY)
    return pl.pallas_call(
        lambda a_ref, other_ref, out_ref: None,
        out_shape=jax.ShapeDtypeStruct(a.shape, a.dtype),
        in_specs=[anywhere, anywhere],
        out_specs=anywhere,
        input_output_aliases={0: 0},
    )(a, other)


def token_half(a, core):
    half = a.shape[0] // 2
    mine = lax.dynamic_slice_in_dim(a, core * half, half, 0)
    others = permute(lax.dynamic_slice_in_dim(a, (1 - core) * half, half, 0), SWAP)
    return jnp.concatenate([mine, others], axis=1)


def for_columns(block):
    return jnp.broadcast_to(block[None], (COLS,) + block.shape)


def gather_columns(copies):
    return lax.all_to_all(copies, "col", 0, 0)


def sum_columns(a):
    return jnp.sum(lax.all_to_all(a, "col", 0, 0).astype(F32), axis=0).astype(BF)


def token_whole(total, core):
    width = total.shape[1] // 2
    others = permute(total[:, width:], SWAP)
    mine = total[:, :width]
    first = core == 0
    return jnp.concatenate([jnp.where(first, mine, others), jnp.where(first, others, mine)], axis=0)


def owned_blocks(a, z):
    per = COLS // ZS
    rows = per * a.shape[1]

    def block(j):
        at = lax.rem(z + j, ZS) * per
        return lax.dynamic_slice_in_dim(a, at, per, 0).reshape(rows, a.shape[2])

    return {p: jnp.concatenate([block(p[0]), block(p[1])], axis=0) for p in PAIRS}


def scatter_rows(blocks, weight, dims):
    part = {}
    for pair in PAIRS:
        both = lax.optimization_barrier(product(blocks[pair], weight, dims))
        if pair == PAIRS[1]:
            made = both
        rows = both.shape[0] // 2
        part[pair[0]], part[pair[1]] = both[:rows], both[rows:]
    half = rows // 2
    up = permute(part[FAR][:half], UP)
    down = permute(part[FAR][half:], DOWN)
    a, b = part[FAR - 1], part[FAR + 1]
    up = permute(jnp.concatenate([plus(a[:half], up), a[half:]], axis=0), UP)
    down = permute(jnp.concatenate([b[:half], plus(b[half:], down)], axis=0), DOWN)
    for j in range(FAR - 2, 0, -1):
        mark = up
        up = permute(plus(part[j], up), UP)
        down = permute(plus(part[ZS - j], down), DOWN)
    return part[0].astype(F32) + up.astype(F32) + down.astype(F32), made, mark


def gather_rows(own):
    half = own.shape[0] // 2
    pieces = [(own, 0, 0)]
    up = down = own
    for j in range(1, FAR):
        up, down = permute(up, UP), permute(down, DOWN)
        pieces += [(up, ZS - j, 0), (down, j, 0)]
    return pieces + [(permute(up[:half], UP), FAR, 0), (permute(down[half:], DOWN), FAR, half)]


def join_and_multiply(pieces, weight, dims, z, first=None):
    block, inner = pieces[0][0].shape
    rows = ZS * block
    outer = weight.shape[dims[0][1][0] ^ 1]
    step = 2 * block

    def kernel(z_ref, *refs):
        piece_refs, weight_ref = refs[: len(pieces)], refs[len(pieces)]
        joined_ref, made_ref = refs[-2:]
        for ref, (piece, j, first) in zip(piece_refs, pieces):
            at = lax.rem(z_ref[0] + j, ZS) * block + first
            count = piece.shape[0]
            joined_ref[pl.ds(pl.multiple_of(at, count), count), :] = ref[...]

        @pl.loop(0, rows // step)
        def _(n):
            these = pl.ds(pl.multiple_of(n * step, step), step)
            made_ref[these, :] = lax.dot_general(
                joined_ref[these, :], weight_ref[...], dims, preferred_element_type=F32
            ).astype(BF)

    vmem = pl.BlockSpec(memory_space=pltpu.VMEM)
    return pl.pallas_call(
        kernel,
        out_shape=(
            jax.ShapeDtypeStruct((rows, inner), BF),
            jax.ShapeDtypeStruct((rows, outer), BF),
        ),
        in_specs=[pl.BlockSpec(memory_space=pltpu.SMEM)] + [vmem] * (len(pieces) + 1)
        + ([] if first is None else [pl.BlockSpec(memory_space=pl.ANY)]),
        out_specs=(vmem, vmem),
        compiler_params=pltpu.CompilerParams(vmem_limit_bytes=40 * 2**20),
        cost_estimate=pl.CostEstimate(
            flops=2 * rows * inner * outer,
            bytes_accessed=2 * (2 * rows * inner + inner * outer + rows * outer),
            transcendentals=0,
        ),
    )(z.reshape(1), *(piece for piece, _, _ in pieces), weight, *([] if first is None else [first]))


def add_halves(mine, others, factor):
    steps = 4
    rows, columns = others.shape[0] // steps, others.shape[1]
    spec = pl.BlockSpec((rows, columns), lambda n: (n, 0))

    def kernel(mine_ref, others_ref, out_ref):
        out_ref[...] = (mine_ref[...] + others_ref[...].astype(F32)) * factor

    return pl.pallas_call(
        kernel,
        out_shape=jax.ShapeDtypeStruct(others.shape, F32),
        grid=(steps,),
        in_specs=[spec, spec],
        out_specs=spec,
        cost_estimate=pl.CostEstimate(flops=0, bytes_accessed=0, transcendentals=0),
    )(mine, others)


def on_device(tokens, w_in, w_out, cotangent):
    row = lax.axis_index("row")
    core, z = lax.rem(row, 2), lax.div(row, 2)
    width = w_in.shape[0]
    half = tokens.shape[0] // 2

    def by_column(a):
        return a.reshape(COLS, half, a.shape[1])

    def by_token(a):
        return a.reshape(COLS * half, a.shape[2])

    x_all = gather_columns(for_columns(token_half(tokens, core)))
    dy_sent = after(for_columns(token_half(cotangent, core)), w_in)
    w_in2 = jnp.concatenate([w_in, permute(w_in, SWAP)], axis=0)
    w_out2 = jnp.concatenate([w_out, permute(w_out, SWAP)], axis=1)
    w_out2_t = after(w_out2.T, w_in2)
    x_all = after(after(x_all, w_out2_t), dy_sent)
    pre, made, mark = scatter_rows(owned_blocks(x_all, z), w_in2, PLAIN)
    hidden, slope = lax.optimization_barrier((gelu_value(pre).astype(BF), gelu_slope(pre)))

    dy_all = after(gather_columns(after(dy_sent, made)), mark)
    grad_hidden, _, _ = scatter_rows(owned_blocks(dy_all, z), w_out2_t, PLAIN)
    grad_pre = lax.optimization_barrier((grad_hidden * slope).astype(BF))

    h_all, made = join_and_multiply(gather_rows(hidden), w_out2, PLAIN, z)
    total = sum_columns(by_column(made))
    mixed = token_whole(total, core)
    dg_all, made = join_and_multiply(gather_rows(grad_pre), w_in2, CONTRACT_COLS, z)
    total = sum_columns(by_column(made))

    factor = 1.0 / math.sqrt(COLS * tokens.shape[0])
    half_in = lax.dot_general(by_token(x_all), dg_all, CONTRACT_ROWS, preferred_element_type=F32)
    grad_w_in = add_halves(half_in, permute(half_in[width:].astype(BF), SWAP), factor)
    half_out = lax.dot_general(
        after(h_all, made), by_token(dy_all), CONTRACT_ROWS, preferred_element_type=F32
    )
    grad_w_out = add_halves(half_out, permute(half_out[:, width:].astype(BF), SWAP), factor)
    grad_tokens = token_whole(after(after(total, grad_w_in), grad_w_out), core)
    return (mixed, grad_tokens, grad_w_in, grad_w_out)


def solution(mesh):
    placed = (P("col", "row"), P("row", "col"), P("col", "row"), P("col", "row"))
    return jax.shard_map(
        on_device,
        mesh=mesh,
        in_specs=placed,
        out_specs=(P("col", "row"), P("col", "row"), P("row", "col"), P("col", "row")),
        check_vma=False,
    )
```
